256 devices in a mesh: dp: 32 (over x, z_hi, core), expert: 8 (over z_lo, y).
Axes of the slice: x: 4, y: 4, z: 8 (z_hi: 4, z_lo: 2; z = z_hi * 2 + z_lo), core: 2. Of those that a mesh axis runs over, the one named last changes fastest.
Arguments:
- grad_output: bfloat16 [32768, 6144], P(('dp', 'expert')), may hold values from -0.59765625 to 0.59765625
- hidden: bfloat16 [32, 8, 8, 48, 1024], P('dp', 'expert'), may hold values from -6 to 6
- probs: bfloat16 [32768, 2], P(('dp', 'expert')), may hold values from 0.099609375 to 0.8984375
- expert_ids: int32 [32768, 2], P(('dp', 'expert')), may hold values from 0 to 7, all different within a row; in each aligned block of 128 rows (0 to 127, 128 to 255, ...) at most 48 rows name the same one
- master: float32 [8, 1024, 6144], P('expert', 'dp'), may hold values from -0.1875 to 0.1875
- first_moment: float32 [8, 1024, 6144], P('expert', 'dp'), may hold values from -12 to 12
- second_moment: float32 [8, 1024, 6144], P('expert', 'dp'), may hold values from 1 to 40
Outputs:
- grad_hidden: bfloat16 [32, 8, 8, 48, 1024], P('dp', 'expert')
- grad_probs: float32 [32768, 2], P(('dp', 'expert'))
- new_master: float32 [8, 1024, 6144], P('expert', 'dp')
- new_first: float32 [8, 1024, 6144], P('expert', 'dp')
- new_second: float32 [8, 1024, 6144], P('expert', 'dp')
The draws below stay inside these ranges and needn't reach their ends.
Inputs may be any that keep to these rules, and one draw needn't show every extreme that they name: `expert_ids`: in the rows of one device (aligned blocks of 128 tokens) each expert is named by at most 48 tokens, a bound that some block reaches; a token's two experts differ.
All inputs are finite; a program needn't handle non-finite values.
Results may differ from the reference program's by a relative error of at most 0.007.
Values may be sent and summed in bfloat16 or wider, within the bound.
A program may use at most 128 MiB of HBM per device.

```python
import math
import jax
import jax.numpy as jnp
import numpy as np
from jax import lax

D = 6144
SLAB = 1024
TOK_DEV = 128
EXPERTS = 8
CAP = 48
TOKENS = 32768
N_DP = 32


def spiked(array, rng, source, target, shards_of, factor):
    def block_of(axis_at):
        return (jnp.arange(array.shape[axis_at]) // (array.shape[axis_at] // shards_of)).reshape((-1,) + (1,) * (array.ndim - 1 - axis_at))

    near = jax.random.permutation(rng, shards_of)[block_of(target)]
    far = (block_of(target) + shards_of // 2) % shards_of
    return jnp.where((block_of(source) == near) | (block_of(source) == far), factor * array, array)


def steps_of(stream_key, shape, shards, smallest, top_value):
    def one(position, parts):
        steps = jax.random.uniform(jax.random.fold_in(jax.random.fold_in(stream_key, 6), position), (parts,), jnp.float32, smallest / len(shards), top_value / len(shards))
        return jnp.repeat(jnp.exp(steps), shape[position] // parts).reshape((-1,) + (1,) * (len(shape) - position - 1))

    level = one(*shards[0])
    for cut in shards[1:]:
        level = level * one(*cut)
    return level


def assign_block(stream_key, own, number, rows, count, top, most, slope):
    order = jax.random.permutation(stream_key, count)
    heavy_load, ordinary = load_shares(count, rows * top, most, slope, True), load_shares(count, rows * top, most, slope, False)
    places = jnp.arange(count)

    def named(lengths, offset_by):
        used = int((lengths > 0).sum())
        fixed = max(1, used // 4)
        shifted = fixed + (places - fixed + offset_by * (used - fixed)) % max(1, count - fixed)
        return jnp.zeros((count,), jnp.int32).at[order[jnp.where(places < fixed, places, shifted)]].set(jnp.asarray(lengths, jnp.int32))

    lengths = jnp.where(number % 4 == 0, named(heavy_load, number // 4), named(ordinary, number - number // 4 - 1))
    mixed = jax.random.permutation(jax.random.fold_in(own, 3), count)
    giver, taker = mixed[0:count // 2 * 2:2], mixed[1:count // 2 * 2:2]
    slack = jnp.minimum(lengths[giver] - 1, most - lengths[taker]) // 2
    slack = jnp.where((giver == order[0]) | (taker == order[0]) | (lengths[taker] == 0), 0, jnp.maximum(slack, 0))
    shifted = jax.random.randint(jax.random.fold_in(own, 4), (count // 2,), 0, 1 << 20) % (slack + 1)
    lengths = lengths.at[giver].add(-shifted).at[taker].add(shifted)
    members = jnp.searchsorted(jnp.cumsum(lengths), jnp.arange(rows * top), side="right").astype(jnp.int32)
    grid = members.reshape(top, rows).T
    grid = grid[jax.random.permutation(jax.random.fold_in(own, 1), rows)]
    offset_by = jax.random.randint(jax.random.fold_in(own, 2), (rows, 1), 0, top)
    return jnp.take_along_axis(grid, (jnp.arange(top)[None, :] + offset_by) % top, axis=1)


def load_shares(amount, total, bound, lean, full):
    portions = [(1 << 20) // math.isqrt(standing ** lean) + 1 for standing in range(1, amount + 1)]
    largest = bound if full else min(bound, max(-(-total // amount), total * portions[0] // sum(portions)))
    least = 1 if total - largest >= amount - 1 else 0
    holding, surplus = [largest] + [least] * (amount - 1), total - largest - least * (amount - 1)
    while surplus > 0:
        candidates = [i for i in range(1, amount) if holding[i] < largest] or [i for i in range(1, amount) if holding[i] < bound]
        mass, left = sum([portions[i] for i in candidates]), surplus
        for i in candidates:
            extra = min(bound - holding[i], max(1, left * portions[i] // mass), surplus)
            holding[i] = holding[i] + extra
            surplus = surplus - extra
    return np.array(holding)


def centred(stream_key, dims, spread, reach, pieces=(), kind=jnp.bfloat16):
    array = spread * jax.random.normal(stream_key, dims, jnp.float32)
    if pieces:
        array = array * steps_of(stream_key, dims, pieces, -0.22, 0.18)
    return jnp.clip(array, -reach, reach).astype(kind)


def bell_draw_with(key, dims, spread, most, split, heavy, kind=jnp.bfloat16):
    array = spread * jax.random.normal(key, dims, jnp.float32)
    if split:
        array = array * steps_of(key, dims, split, -0.22, 0.18)
    return jnp.clip(spiked(array, jax.random.fold_in(key, 3), *heavy), -most, most).astype(kind)


def setup_inputs(seed: int = 0) -> dict:
    key_list = jax.random.split(jax.random.key(seed), 8)
    grad_output = centred(key_list[0], (TOKENS, D), 0.1, 0.59765625, ((0, 256),))
    hidden = bell_draw_with(key_list[1], (N_DP, EXPERTS, EXPERTS, CAP, SLAB), 1.0, 6.0, ((0, 32), (1, 8)), (0, 4, 32, 2.75))
    probs = jnp.clip(0.099609375 + 0.7988281 * jax.random.uniform(key_list[2], (TOKENS, 2), jnp.float32) ** steps_of(key_list[2], (TOKENS, 2), ((0, 256),), -0.2, 0.2), 0.099609375, 0.8984375).astype(jnp.bfloat16)
    expert_ids_keys = jax.random.split(jax.random.fold_in(key_list[3], 1), TOKENS // TOK_DEV)
    expert_ids_turns = jax.random.permutation(jax.random.fold_in(key_list[3], 3), TOKENS // TOK_DEV)
    expert_ids = jax.vmap(lambda own, number: assign_block(jax.random.fold_in(key_list[3], 2), own, number, TOK_DEV, EXPERTS, 2, CAP, 2))(expert_ids_keys, expert_ids_turns).reshape((TOKENS, 2))
    master = centred(key_list[4], (EXPERTS, SLAB, D), SLAB ** -0.5, 0.1875, ((0, 8), (1, 32)), jnp.float32)
    first_moment = centred(key_list[5], (EXPERTS, SLAB, D), 2.0, 12.0, ((0, 8), (1, 32)), jnp.float32)
    second_moment = jnp.clip(jnp.exp(math.log(40.0) - 3.6888795 * jax.random.uniform(key_list[6], (EXPERTS, SLAB, D), jnp.float32) ** steps_of(key_list[6], (EXPERTS, SLAB, D), ((0, 8), (1, 32)), -0.2, 0.2)), 1.0, 40.0)
    return dict(grad_output=grad_output, hidden=hidden, probs=probs, expert_ids=expert_ids, master=master, first_moment=first_moment, second_moment=second_moment)


def slot_numbers(id_rows):
    onehot = (id_rows[..., None] == jnp.arange(EXPERTS, dtype=jnp.int32)).astype(jnp.int32)
    before = jnp.cumsum(onehot, axis=-2) - onehot
    return lax.optimization_barrier(jnp.sum(before * onehot, axis=-1)).astype(jnp.int32)

def place_rows(id_row, slot_row, token_rows, prob_row):
    sent = jnp.zeros((EXPERTS, CAP, D), jnp.bfloat16).at[id_row, slot_row].set(token_rows)
    sent_prob = jnp.zeros((EXPERTS, CAP), jnp.bfloat16).at[id_row, slot_row].set(prob_row)
    return (sent, sent_prob)

def pick_back(table, id_row, slot_row):
    return table[id_row, slot_row]

def reference(grad_output, hidden, probs, expert_ids, master, first_moment, second_moment):
    grads_in = grad_output.reshape(N_DP, EXPERTS, TOK_DEV, D)
    ids_in = expert_ids.reshape(N_DP, EXPERTS, 2 * TOK_DEV)
    probs_in = probs.reshape(N_DP, EXPERTS, 2 * TOK_DEV)
    weights_f = master.astype(jnp.bfloat16).astype(jnp.float32)
    pair_token = (jnp.arange(2 * TOK_DEV, dtype=jnp.int32) // 2).astype(jnp.int32)

    def group(total, inputs):
        grad_group, id_group, prob_group, hidden_group = inputs
        slots = slot_numbers(id_group)
        token_rows = grad_group[:, pair_token]
        sent, sent_prob = jax.vmap(place_rows)(id_group, slots, token_rows, prob_group)
        routed = jnp.transpose(sent, (1, 0, 2, 3))
        weight = jnp.transpose(sent_prob, (1, 0, 2))
        scaled = (weight.astype(jnp.float32)[..., None] * routed.astype(jnp.float32)).astype(jnp.bfloat16)
        hidden_f = hidden_group.astype(jnp.float32)
        scaled_f = scaled.astype(jnp.float32)
        expert_out = jnp.einsum('ejcs,esd->ejcd', hidden_f, weights_f)
        row_grad = lax.optimization_barrier(jnp.sum(routed.astype(jnp.float32) * expert_out, axis=-1))
        grad_hid = jnp.einsum('ejcd,esd->ejcs', scaled_f, weights_f).astype(jnp.bfloat16)
        partial_sum = jnp.einsum('ejcs,ejcd->esd', hidden_f, scaled_f).astype(jnp.bfloat16)
        total = total + partial_sum.astype(jnp.float32)
        back = jnp.transpose(row_grad, (1, 0, 2))
        pair_grad = jax.vmap(pick_back)(back, id_group, slots)
        return (total, (grad_hid, pair_grad))
    start_total = jnp.zeros((EXPERTS, SLAB, D), jnp.float32)
    grad, (grad_hidden, pair_grads) = lax.scan(group, start_total, (grads_in, ids_in, probs_in, hidden))
    grad_probs = pair_grads.reshape(TOKENS, 2)
    new_first = 0.9 * first_moment + 0.1 * grad
    new_second = 0.95 * second_moment + 0.05 * grad * grad
    first_hat = new_first / (1.0 - 0.9 ** 50)
    second_hat = new_second / (1.0 - 0.95 ** 50)
    new_master = master - 0.0003 * (first_hat / (jnp.sqrt(second_hat) + 1e-08) + 0.1 * master)
    return (grad_hidden, grad_probs, new_master, new_first, new_second)
```

```python
import jax
import jax.numpy as jnp
from jax import lax
from jax.experimental import pallas as pl
from jax.experimental.pallas import tpu as pltpu
from jax.sharding import PartitionSpec as P

MESH = pl.DeviceIdType.MESH
F32 = jnp.float32
BF16 = jnp.bfloat16
CAP = 48
WIDTHS = [128, 128, 256, 256, 256, 256, 128, 128]


def kernel(
    ids_ref, prob_ref, g_ref, hid_hbm, mas_hbm,
    gh_ref, gp_ref, gr_ref,
    INF, INE, T, SO, SB, RB, PC, HID, MAS, HQ, HT, WB, WQ, PX, PO, XR, ZS, ZR, FS, FR,
    GS1, GR1, GO1, GX, GR2, GO, RG, BK,
    l_s, is_s, is_r, ie_s, ie_r, iz_s, iz_r, q_s, q_r, z_s, z_r, y_s, y_r, y_l, x_s, x_r, zh_s, zh_r,
    f_s, f_r, h_s, h_r, w_s, w_r, wz_s, wz_r, wf_s, wf_r, wx_s, wx_r, g1_s, g1_r, g2_s, g2_r, b_s, b_r,
):
    QW = RB.shape[4]
    NC = len(WIDTHS)
    OFF = [sum(WIDTHS[:k]) for k in range(NC)]
    dp = lax.axis_index("dp")
    ex = lax.axis_index("expert")
    x, zh, c = dp // 8, (dp // 2) % 4, dp % 2
    zl, y = ex // 4, ex % 4
    px, xl = x // 2, x % 2
    h = (xl + px) % 2
    s = h * 2 + c
    xp = px * 2 + (1 - xl)

    def dev(x_, zh_, c_, zl_, y_):
        return ((x_ * 4 + zh_) * 2 + c_, zl_ * 4 + y_)

    mate_dev = [dev(x, zh, 1 - c, zl, y), dev(xp, zh, c, zl, y), dev(xp, zh, 1 - c, zl, y)]
    mate_s = [h * 2 + (1 - c), (1 - h) * 2 + c, (1 - h) * 2 + (1 - c)]
    mate_xl = [xl, 1 - xl, 1 - xl]
    mate_c = [1 - c, c, 1 - c]
    xc_dev = dev(3 - x, zh, c, zl, y)
    zl_dev = dev(x, zh, c, 1 - zl, y)
    y_dev = [dev(x, zh, c, zl, (y + d) % 4) for d in (1, 2, 3)]
    yz_dev = [dev(x, zh, c, 1 - zl, (y + d) % 4) for d in (1, 2, 3)]
    zh_dev = [dev(x, (zh + d) % 4, c, zl, y) for d in (1, 2, 3)]
    peer_dev = y_dev + [zl_dev] + yz_dev
    peer_ex = [zl * 4 + (y + d) % 4 for d in (1, 2, 3)] + [
        (1 - zl) * 4 + (y + d) % 4 for d in (0, 1, 2, 3)
    ]

    started, got, own = [], [], []

    class Copy:
        def __init__(self, key, src, dst, ssem, rsem, to):
            self.key = key
            self.d = pltpu.make_async_remote_copy(
                src_ref=src, dst_ref=dst, send_sem=ssem, recv_sem=rsem, device_id=to,
                device_id_type=MESH,
            )

        def start(self):
            assert self.key not in started
            started.append(self.key)
            self.d.start()

        def wait_recv(self):
            assert self.key not in got
            got.append(self.key)
            self.d.wait_recv()

        def wait_send(self):
            self.d.wait_send()

    def ck(k):
        return pl.ds(OFF[k], WIDTHS[k])

    def cols(start, size):
        return pl.ds(pl.multiple_of(start, 128), size)

    def info_mate(r):
        ref = INF.at[zl, s]
        return Copy((info_mate, r), ref, ref, is_s.at[r], is_r.at[r], mate_dev[r])

    def info_peer(i):
        ref = INE.at[ex]
        return Copy((info_peer, i), ref, ref, ie_s.at[i], ie_r.at[i], peer_dev[i])

    def info_z():
        ref = INF.at[zl]
        return Copy((info_z,), ref, ref, iz_s, iz_r, zl_dev)

    def q_copy(k, r):
        src = g_ref.at[:, cols(mate_s[r] * QW + OFF[k], WIDTHS[k])]
        return Copy((q_copy, k, r), src, T.at[zl, s, :, ck(k)], q_s.at[k, r], q_r.at[k, r], mate_dev[r])

    def z_copy(k):
        ref = T.at[zl, :, :, ck(k)]
        return Copy((z_copy, k), ref, ref, z_s.at[k], z_r.at[k], zl_dev)

    def y_copy(k, o, d):
        zz = zl if o == 0 else 1 - zl
        return Copy(
            (y_copy, k, o, d), SB.at[zz, (y + d) % 4, :, :, ck(k)], RB.at[:, zz, y, :, ck(k)],
            y_s.at[k, o, d - 1], y_r.at[k, o, d - 1], y_dev[d - 1],
        )

    def y_own(k, o):
        zz = zl if o == 0 else 1 - zl
        return pltpu.make_async_copy(
            SB.at[zz, y, :, :, ck(k)], RB.at[:, zz, y, :, ck(k)], y_l.at[k, o]
        )

    def x_copy(k):
        return Copy((x_copy, k), PX.at[:, ck(k)], XR.at[:, ck(k)], x_s.at[k], x_r.at[k], xc_dev)

    def zh_copy(k, d):
        return Copy(
            (zh_copy, k, d), ZS.at[(zh + d) % 4, :, :, ck(k)], ZR.at[d - 1, :, :, ck(k)],
            zh_s.at[k, d - 1], zh_r.at[k, d - 1], zh_dev[d - 1],
        )

    def f_copy(k, r):
        return Copy(
            (f_copy, k, r), FS.at[mate_xl[r], mate_c[r], :, ck(k)], FR.at[s, :, ck(k)],
            f_s.at[k, r], f_r.at[k, r], mate_dev[r],
        )

    def h_copy(i):
        ref = HQ.at[mate_s[1] if i == 2 else s]
        return Copy((h_copy, i), ref, ref, h_s.at[i], h_r.at[i], mate_dev[1 if i == 1 else 0])

    def w_copy(r):
        src = WB.at[:, cols(mate_s[r] * QW, QW)]
        return Copy((w_copy, r), src, WQ.at[x, zh, c], w_s.at[r], w_r.at[r], mate_dev[r])

    half = QW // 2
    pair = pl.ds(px * 2, 2)

    def wz_copy(i):
        ref = WQ.at[pair, zh]
        return Copy((wz_copy, i), ref, ref, wz_s.at[i], wz_r.at[i], zh_dev[0 if i == 0 else 2])

    def wf_copy(i):
        blk = (zh + 3) % 4 if i == 0 else (zh + 1) % 4
        ref = WQ.at[pair, blk, :, :, pl.ds(i * half, half)]
        return Copy((wf_copy, i), ref, ref, wf_s.at[i], wf_r.at[i], zh_dev[0 if i == 0 else 2])

    def wx_copy(d):
        ref = WQ.at[pair, (zh + d) % 4]
        return Copy((wx_copy, d), ref, ref, wx_s.at[d], wx_r.at[d], xc_dev)

    NB = 4
    BW = 1024 // NB

    def slab_cols(u):
        n = (px * 2 if u < 2 else 2 - px * 2) + u % 2
        return cols(n * BW, BW)

    def g1_copy(i, u):
        sl = slab_cols(u)
        return Copy(
            (g1_copy, i, u), GS1.at[i, :, sl], GR1.at[i, :, sl], g1_s.at[i, u], g1_r.at[i, u], mate_dev[0]
        )

    def g2_copy(u):
        sl = slab_cols(u)
        return Copy((g2_copy, u), GX.at[:, sl], GR2.at[:, sl], g2_s.at[u], g2_r.at[u], mate_dev[1])

    def b_copy(i):
        return Copy((b_copy, i), RG.at[peer_ex[i]], BK.at[ex], b_s.at[i], b_r.at[i], peer_dev[i])

    def loads():
        return [
            pltpu.make_async_copy(g_ref.at[:, cols(s * QW, QW)], T.at[zl, s], l_s.at[0]),
            pltpu.make_async_copy(mas_hbm, MAS, l_s.at[1]),
            pltpu.make_async_copy(hid_hbm, HID, l_s.at[2]),
        ]

    barrier = pltpu.get_barrier_semaphore()
    everyone = mate_dev + [xc_dev] + peer_dev + zh_dev
    for to in everyone:
        pl.semaphore_signal(barrier, inc=1, device_id=to, device_id_type=MESH)
    for cp in loads():
        cp.start()

    sub = lax.broadcasted_iota(jnp.int32, (8, 128), 0).astype(F32)
    ids0, ids1 = ids_ref[0:1, :].astype(F32), ids_ref[1:2, :].astype(F32)
    prob = prob_ref[...].astype(F32)
    oh0 = (sub == ids0).astype(F32)
    oh1 = (sub == ids1).astype(F32)
    tri = (
        lax.broadcasted_iota(jnp.int32, (128, 128), 0) < lax.broadcasted_iota(jnp.int32, (128, 128), 1)
    ).astype(BF16)
    before = jnp.dot((oh0 + oh1).astype(BF16), tri, preferred_element_type=F32)
    t0 = ids0 * float(CAP) + jnp.sum(oh0 * before, axis=0, keepdims=True)
    t1 = ids1 * float(CAP) + jnp.sum(oh1 * before, axis=0, keepdims=True)
    mine = jnp.where(
        sub == 0.0, t0, jnp.where(sub == 1.0, t1, jnp.where(sub == 2.0, prob[0:1, :], prob[1:2, :]))
    )
    INF[zl, s] = mine
    INE[ex] = mine

    pl.semaphore_wait(barrier, len(everyone))

    def stage_info():
        for r in (1, 2, 0):
            info_mate(r).start()

    def stage_peer():
        for i in range(7):
            info_peer(i).start()

    def stage_w0():
        loads()[1].wait()
        WB[...] = MAS[...].astype(BF16)
        for r in (1, 2, 0):
            w_copy(r).start()
        WQ[x, zh, c] = WB[:, cols(s * QW, QW)]

    def stage_q(k):
        for r in (1, 2, 0):
            q_copy(k, r).start()

    def onehot(zz):
        rows = lax.broadcasted_iota(jnp.int32, (4 * CAP, 128), 0) + zl * (4 * CAP)
        rows = rows.astype(F32)
        for ss in range(4):
            inf = INF[zz, ss]
            hit = (rows == inf[0:1, :]) | (rows == inf[1:2, :])
            SO[zz, ss] = jnp.where(hit, 1.0, 0.0).astype(BF16)

    def stage_o0():
        for r in range(3):
            info_mate(r).wait_recv()
        info_z().start()
        onehot(zl)

    def stage_o1():
        info_z().wait_recv()
        onehot(1 - zl)

    def stage_h():
        for i in range(7):
            info_peer(i).wait_recv()
        loads()[2].wait()
        rows = (lax.broadcasted_iota(jnp.int32, (CAP, 128), 0) + ex * CAP).astype(F32)
        for j in range(8):
            inf = INE[j]
            w = jnp.where(rows == inf[0:1, :], inf[2:3, :], 0.0) + jnp.where(
                rows == inf[1:2, :], inf[3:4, :], 0.0
            )
            p = jnp.sum(w, axis=1, keepdims=True)
            PC[j * CAP:(j + 1) * CAP, :] = jnp.broadcast_to(p, (CAP, 128))
            HQ[s, j * CAP:(j + 1) * CAP, :] = (
                HID[j * CAP:(j + 1) * CAP, :].astype(F32) * p
            ).astype(BF16)
        h_copy(1).start()
        h_copy(0).start()

    def stage_hf():
        h_copy(1).wait_recv()
        h_copy(2).start()

    def stage_ht():
        h_copy(0).wait_recv()
        h_copy(2).wait_recv()
        for ss in range(4):
            HT[:, ss * 384:(ss + 1) * 384] = HQ[ss].T

    def stage_b(k):
        for r in range(3):
            q_copy(k, r).wait_recv()
        if k == 0:
            loads()[0].wait()
        z_copy(k).start()

    def dispatch(k, o):
        zz = zl if o == 0 else 1 - zl
        for ss in range(4):
            out = jnp.dot(SO[zz, ss], T[zz, ss, :, ck(k)], preferred_element_type=F32).astype(BF16)
            for yy in range(4):
                SB[zz, yy, ss, :, ck(k)] = out[yy * CAP:(yy + 1) * CAP]
        for d in (2, 1, 3):
            y_copy(k, o, d).start()
        y_own(k, o).start()
        own.append((k, o))

    def stage_a(k):
        dispatch(k, 0)

    def stage_c(k):
        z_copy(k).wait_recv()
        dispatch(k, 1)

    def stage_d(k):
        for o in range(2):
            y_own(k, o).wait()
            own.remove((k, o))
            for d in (1, 2, 3):
                y_copy(k, o, d).wait_recv()
        rb = RB[:, :, :, :, ck(k)].reshape(4 * 384, WIDTHS[k])
        there = jnp.dot(HT[pl.ds((1 - px) * 512, 512), :], rb, preferred_element_type=F32)
        PX[:, ck(k)] = there.astype(BF16)
        x_copy(k).start()
        PO[:, ck(k)] = jnp.dot(HT[pl.ds(px * 512, 512), :], rb, preferred_element_type=F32)

    def stage_e(k):
        x_copy(k).wait_recv()
        tot = (PO[:, ck(k)] + XR[:, ck(k)].astype(F32)).astype(BF16).reshape(2, 4, 64, WIDTHS[k])
        for a in range(2):
            for b in range(4):
                ZS[b, a, :, ck(k)] = tot[a, b]
        for d in (2, 1, 3):
            zh_copy(k, d).start()

    def stage_f(k):
        for d in (1, 2, 3):
            zh_copy(k, d).wait_recv()
        tot = ZS[zh, :, :, ck(k)].astype(F32)
        for d in range(3):
            tot = tot + ZR[d, :, :, ck(k)].astype(F32)
        FS[:, :, :, ck(k)] = tot.astype(BF16).reshape(2, 2, 32, WIDTHS[k])
        for r in (1, 2, 0):
            f_copy(k, r).start()
        FR[s, :, ck(k)] = FS[xl, c, :, ck(k)]

    def stage_w1():
        for r in range(3):
            w_copy(r).wait_recv()
        wx_copy(0).start()
        for i in range(2):
            wz_copy(i).start()

    def stage_w2():
        for i in range(2):
            wz_copy(i).wait_recv()
            wf_copy(i).start()
        wx_copy(3).start()
        wx_copy(1).start()

    def stage_w3():
        for i in range(2):
            wf_copy(i).wait_recv()
        wx_copy(2).start()

    def stage_w4():
        for d in range(4):
            wx_copy(d).wait_recv()

    nt = (((1,), (1,)), ((), ()))

    def gdot(row, n):
        wn = WQ[n].reshape(BW, QW)
        return lax.dot_general(RB[row].reshape(384, QW), wn, nt, preferred_element_type=F32)

    def blk(i):
        return [i * 2, i * 2 + 1], [(px * 2 if i == 0 else 2 - px * 2) + a for a in range(2)]

    def stage_g1(i):
        for u, n in zip(*blk(i)):
            sl = cols(n * BW, BW)
            GS1[0, :, sl] = gdot(mate_s[2], n).astype(BF16)
            g1_copy(0, u).start()
            GO1[:, sl] = gdot(mate_s[1], n)

    def stage_g2(i):
        for u, n in zip(*blk(i)):
            sl = cols(n * BW, BW)
            g1_copy(0, u).wait_recv()
            GX[:, sl] = (GO1[:, sl] + GR1[0, :, sl].astype(F32)).astype(BF16)
            g2_copy(u).start()

    def stage_g3():
        for i in range(2):
            for u, n in zip(*blk(i)):
                sl = cols(n * BW, BW)
                GS1[1, :, sl] = gdot(mate_s[0], n).astype(BF16)
                g1_copy(1, u).start()
                GO[:, sl] = gdot(s, n)

    def stage_gr():
        for n in range(NB):
            g1_copy(1, n).wait_recv()
        for n in range(NB):
            g2_copy(n).wait_recv()
        for j in range(8):
            sl = slice(j * CAP, (j + 1) * CAP)
            tot = GO[sl, :] + GR1[1, sl, :].astype(F32) + GR2[sl, :].astype(F32)
            rg = jnp.sum(HID[sl, :].astype(F32) * tot, axis=1, keepdims=True)
            RG[j] = jnp.broadcast_to(rg, (CAP, 128))
            gh_ref[sl, :] = (tot * PC[sl, 0:1]).astype(BF16)
        for i in range(7):
            b_copy(i).start()
        BK[ex] = RG[ex]

    def stage_gp():
        for i in range(7):
            b_copy(i).wait_recv()
        inf = INE[ex]
        acc0 = jnp.zeros((1, 128), F32)
        acc1 = jnp.zeros((1, 128), F32)
        base = lax.broadcasted_iota(jnp.int32, (CAP, 128), 0).astype(F32)
        for e in range(8):
            rows = base + float(e * CAP)
            acc0 += jnp.sum(jnp.where(rows == inf[0:1, :], BK[e], 0.0), axis=0, keepdims=True)
            acc1 += jnp.sum(jnp.where(rows == inf[1:2, :], BK[e], 0.0), axis=0, keepdims=True)
        gp_ref[0:1, :] = acc0
        gp_ref[1:2, :] = acc1

    def stage_end():
        for k in range(NC):
            for r in range(3):
                f_copy(k, r).wait_recv()
        for q in range(4):
            gr_ref[:, q * QW:(q + 1) * QW] = FR[q]

    fns = dict(
        info=stage_info, peer=stage_peer, w0=stage_w0, q=stage_q, o0=stage_o0, o1=stage_o1, h=stage_h, hf=stage_hf, ht=stage_ht, a=stage_a, b=stage_b,
        c=stage_c, d=stage_d, e=stage_e, f=stage_f, w1=stage_w1, w2=stage_w2, w3=stage_w3,
        w4=stage_w4, g1=stage_g1, g2=stage_g2, g3=stage_g3, gr=stage_gr, gp=stage_gp, end=stage_end,
    )
    for name, *k in ORDER:
        fns[name](*k)

    for k in own:
        y_own(*k).wait()
    names = [item[0] for item in ORDER]
    for i, name in enumerate(("b", "w0", "h")):
        if name not in names:
            loads()[i].wait()
    for fn, *a in started:
        if (fn, *a) not in got:
            fn(*a).wait_recv()
        fn(*a).wait_send()


ORDER = [
    ("q", 0), ("info",), ("q", 1), ("w0",), ("q", 2), ("b", 0), ("b", 1), ("peer",), ("q", 3),
    ("o0",), ("w1",), ("q", 4), ("q", 5), ("a", 1), ("q", 6), ("b", 2), ("b", 3), ("a", 3),
    ("o1",), ("a", 2), ("b", 4), ("c", 1), ("h",), ("b", 5), ("b", 6), ("a", 5), ("a", 0),
    ("c", 0), ("a", 4), ("w2",), ("c", 2), ("hf",), ("c", 3), ("ht",), ("q", 7), ("a", 6),
    ("d", 1), ("d", 2), ("d", 3), ("c", 5), ("b", 7), ("d", 0), ("c", 6), ("a", 7), ("c", 4),
    ("e", 2), ("w3",), ("e", 3), ("d", 6), ("e", 0), ("c", 7), ("d", 5), ("d", 4), ("e", 1),
    ("d", 7), ("g1", 0), ("g2", 0), ("e", 6), ("w4",), ("g1", 1), ("e", 5), ("g2", 1), ("e", 4),
    ("f", 3), ("g3",), ("e", 7), ("f", 6), ("f", 5), ("f", 0), ("f", 1), ("f", 2), ("gr",),
    ("f", 4), ("f", 7), ("gp",), ("end",),
]


def per_device(grad_output, hidden, probs, expert_ids, master, first_moment, second_moment):
    width = grad_output.shape[1]
    qw = width // 4
    nc = len(WIDTHS)
    slab = hidden.shape[4]
    rows = hidden.shape[2] * hidden.shape[3]
    vm = pl.BlockSpec(memory_space=pltpu.VMEM)
    hbm = pl.BlockSpec(memory_space=pl.ANY)
    dma = pltpu.SemaphoreType.DMA
    scratch = [
        pltpu.VMEM((2, 4, 8, 128), F32),
        pltpu.VMEM((8, 8, 128), F32),
        pltpu.VMEM((2, 4, 128, qw), BF16),
        pltpu.VMEM((2, 4, 4 * CAP, 128), BF16),
        pltpu.VMEM((2, 4, 4, CAP, qw), BF16),
        pltpu.VMEM((4, 2, 4, CAP, qw), BF16),
        pltpu.VMEM((rows, 128), F32),
        pltpu.VMEM((rows, slab), BF16),
        pltpu.VMEM((32, width), F32),
        pltpu.VMEM((4, rows, slab), BF16),
        pltpu.VMEM((slab, 4 * rows), BF16),
        pltpu.VMEM((32, width), BF16),
        pltpu.VMEM((4, 4, 2, 32, qw), BF16),
        pltpu.VMEM((512, qw), BF16),
        pltpu.VMEM((512, qw), F32),
        pltpu.VMEM((512, qw), BF16),
        pltpu.VMEM((4, 2, 64, qw), BF16),
        pltpu.VMEM((3, 2, 64, qw), BF16),
        pltpu.VMEM((2, 2, 32, qw), BF16),
        pltpu.VMEM((4, 32, qw), BF16),
        pltpu.VMEM((2, rows, slab), BF16),
        pltpu.VMEM((2, rows, slab), BF16),
        pltpu.VMEM((rows, slab), F32),
        pltpu.VMEM((rows, slab), BF16),
        pltpu.VMEM((rows, slab), BF16),
        pltpu.VMEM((rows, slab), F32),
        pltpu.VMEM((8, CAP, 128), F32),
        pltpu.VMEM((8, CAP, 128), F32),
        dma((3,)),
        dma((3,)), dma((3,)), dma((7,)), dma((7,)), dma, dma,
        dma((nc, 3)), dma((nc, 3)), dma((nc,)), dma((nc,)),
        dma((nc, 2, 3)), dma((nc, 2, 3)), dma((nc, 2)),
        dma((nc,)), dma((nc,)), dma((nc, 3)), dma((nc, 3)), dma((nc, 3)), dma((nc, 3)),
        dma((3,)), dma((3,)), dma((3,)), dma((3,)),
        dma((2,)), dma((2,)), dma((2,)), dma((2,)), dma((4,)), dma((4,)),
        dma((2, 4)), dma((2, 4)), dma((4,)), dma((4,)), dma((7,)), dma((7,)),
    ]
    gh, gp, gr = pl.pallas_call(
        kernel,
        out_shape=(
            jax.ShapeDtypeStruct((rows, slab), BF16),
            jax.ShapeDtypeStruct((2, 128), F32),
            jax.ShapeDtypeStruct((32, width), BF16),
        ),
        in_specs=[vm, vm, hbm, hbm, hbm],
        out_specs=(vm, vm, vm),
        scratch_shapes=scratch,
        compiler_params=pltpu.CompilerParams(
            collective_id=0, has_side_effects=True, vmem_limit_bytes=60 * 1024 * 1024
        ),
        cost_estimate=pl.CostEstimate(
            flops=10 * 10**9, bytes_accessed=8 * 10**6, transcendentals=0
        ),
    )(expert_ids.T, probs.T, grad_output, hidden.reshape(rows, slab), master.reshape(32, width))
    grad_hidden = gh.reshape(hidden.shape)
    grad_probs = gp.T
    grad = gr.astype(F32).reshape(master.shape)
    new_first = 0.9 * first_moment + 0.1 * grad
    new_second = 0.95 * second_moment + 0.05 * grad * grad
    first_hat = new_first / (1.0 - 0.9**50)
    second_hat = new_second / (1.0 - 0.95**50)
    new_master = master - 0.0003 * (first_hat / (jnp.sqrt(second_hat) + 1e-08) + 0.1 * master)
    return (grad_hidden, grad_probs, new_master, new_first, new_second)


def solution(mesh):
    in_specs = (
        P(("dp", "expert"), None),
        P("dp", "expert", None, None, None),
        P(("dp", "expert"), None),
        P(("dp", "expert"), None),
        P("expert", "dp", None),
        P("expert", "dp", None),
        P("expert", "dp", None),
    )
    out_specs = (
        P("dp", "expert", None, None, None),
        P(("dp", "expert"), None),
        P("expert", "dp", None),
        P("expert", "dp", None),
        P("expert", "dp", None),
    )
    return jax.shard_map(
        per_device, mesh=mesh, in_specs=in_specs, out_specs=out_specs, check_vma=False
    )
```

```python
import jax
import jax.numpy as jnp
from jax import lax
from jax.experimental import pallas as pl
from jax.experimental.pallas import tpu as pltpu
from jax.sharding import PartitionSpec as P

MESH = pl.DeviceIdType.MESH
F32 = jnp.float32
BF16 = jnp.bfloat16
CAP = 48
RING = [0, 1, 2, 3, 4, 5]
WIDTHS = [128, 128, 256, 256, 256, 256, 128, 128]


def kernel(
    ids_ref, prob_ref, g_ref, hid_hbm, mas_hbm,
    gh_ref, gp_ref, gr_ref,
    INF, INE, T, SO, SB, RB, PC, HID, MAS, HQ, HT, WB, WQ, PX, PO, XR, ZS, ZR, ZH, FS, FR,
    GS1, GR1, GO1, GX, GR2, GO, RG, BK,
    l_s, is_s, is_r, ie_s, ie_r, iz_s, iz_r, q_s, q_r, z_s, z_r, y_s, y_r, y_l, x_s, x_r, zh_s, zh_r, zn_s, zn_r, za_s, za_r,
    f_s, f_r, h_s, h_r, w_s, w_r, wz_s, wz_r, wf_s, wf_r, wx_s, wx_r, wp_s, wp_r, g1_s, g1_r, g2_s, g2_r, b_s, b_r,
):
    QW = RB.shape[4]
    NC = len(WIDTHS)
    OFF = [sum(WIDTHS[:k]) for k in range(NC)]
    dp = lax.axis_index("dp")
    ex = lax.axis_index("expert")
    x, zh, c = dp // 8, (dp // 2) % 4, dp % 2
    zl, y = ex // 4, ex % 4
    px, xl = x // 2, x % 2
    h = (xl + px) % 2
    s = h * 2 + c
    xp = px * 2 + (1 - xl)

    def dev(x_, zh_, c_, zl_, y_):
        return ((x_ * 4 + zh_) * 2 + c_, zl_ * 4 + y_)

    mate_dev = [dev(x, zh, 1 - c, zl, y), dev(xp, zh, c, zl, y), dev(xp, zh, 1 - c, zl, y)]
    mate_s = [h * 2 + (1 - c), (1 - h) * 2 + c, (1 - h) * 2 + (1 - c)]
    mate_xl = [xl, 1 - xl, 1 - xl]
    mate_c = [1 - c, c, 1 - c]
    xc_dev = dev(3 - x, zh, c, zl, y)
    zl_dev = dev(x, zh, c, 1 - zl, y)
    y_dev = [dev(x, zh, c, zl, (y + d) % 4) for d in (1, 2, 3)]
    yz_dev = [dev(x, zh, c, 1 - zl, (y + d) % 4) for d in (1, 2, 3)]
    zh_dev = [dev(x, (zh + d) % 4, c, zl, y) for d in (1, 2, 3)]
    peer_dev = y_dev + [zl_dev] + yz_dev
    peer_ex = [zl * 4 + (y + d) % 4 for d in (1, 2, 3)] + [
        (1 - zl) * 4 + (y + d) % 4 for d in (0, 1, 2, 3)
    ]

    started, got, sent, own = [], [], [], []

    class Copy:
        def __init__(self, key, src, dst, ssem, rsem, to):
            self.key = key
            self.d = pltpu.make_async_remote_copy(
                src_ref=src, dst_ref=dst, send_sem=ssem, recv_sem=rsem, device_id=to,
                device_id_type=MESH,
            )

        def start(self):
            assert self.key not in started
            started.append(self.key)
            self.d.start()

        def wait_recv(self):
            assert self.key not in got
            got.append(self.key)
            self.d.wait_recv()

        def wait_send(self):
            assert self.key in started and self.key not in sent
            sent.append(self.key)
            self.d.wait_send()

    def ck(k):
        return pl.ds(OFF[k], WIDTHS[k])

    def cols(start, size):
        return pl.ds(pl.multiple_of(start, 128), size)

    def info_mate(r):
        ref = INF.at[zl, s]
        return Copy((info_mate, r), ref, ref, is_s.at[r], is_r.at[r], mate_dev[r])

    def info_peer(i):
        ref = INE.at[ex]
        return Copy((info_peer, i), ref, ref, ie_s.at[i], ie_r.at[i], peer_dev[i])

    def info_z():
        ref = INF.at[zl]
        return Copy((info_z,), ref, ref, iz_s, iz_r, zl_dev)

    def q_copy(k, r):
        src = g_ref.at[:, cols(mate_s[r] * QW + OFF[k], WIDTHS[k])]
        return Copy((q_copy, k, r), src, T.at[zl, s, :, ck(k)], q_s.at[k, r], q_r.at[k, r], mate_dev[r])

    def z_copy(k):
        ref = T.at[zl, :, :, ck(k)]
        return Copy((z_copy, k), ref, ref, z_s.at[k], z_r.at[k], zl_dev)

    def y_copy(k, o, d):
        zz = zl if o == 0 else 1 - zl
        return Copy(
            (y_copy, k, o, d), SB.at[zz, (y + d) % 4, :, :, ck(k)], RB.at[:, zz, y, :, ck(k)],
            y_s.at[k, o, d - 1], y_r.at[k, o, d - 1], y_dev[d - 1],
        )

    def y_own(k, o):
        zz = zl if o == 0 else 1 - zl
        return pltpu.make_async_copy(
            SB.at[zz, y, :, :, ck(k)], RB.at[:, zz, y, :, ck(k)], y_l.at[k, o]
        )

    def x_copy(k):
        return Copy((x_copy, k), PX.at[:, ck(k)], XR.at[:, ck(k)], x_s.at[k], x_r.at[k], xc_dev)

    def zh_copy(k, d):
        return Copy(
            (zh_copy, k, d), ZS.at[(zh + d) % 4, :, :, ck(k)], ZR.at[d - 1, :, :, ck(k)],
            zh_s.at[k, d - 1], zh_r.at[k, d - 1], zh_dev[d - 1],
        )

    ring_dev = [zh_dev[0], zh_dev[2]]

    def zr_copy(k, i):
        return Copy(
            (zr_copy, k, i), ZS.at[(zh + 2) % 4, i, :, ck(k)], ZH.at[i, :, ck(k)],
            zh_s.at[k, i], zh_r.at[k, i], ring_dev[i],
        )

    def zn_copy(k, i):
        return Copy(
            (zn_copy, k, i), ZS.at[(zh + 1 + 2 * i) % 4, 1 - i, :, ck(k)], ZR.at[i, 1 - i, :, ck(k)],
            zn_s.at[k, i], zn_r.at[k, i], ring_dev[i],
        )

    def za_copy(k, i):
        return Copy(
            (za_copy, k, i), ZS.at[(zh + 1 + 2 * i) % 4, i, :, ck(k)], ZR.at[i, i, :, ck(k)],
            za_s.at[k, i], za_r.at[k, i], ring_dev[i],
        )

    def f_copy(k, r):
        return Copy(
            (f_copy, k, r), FS.at[mate_xl[r], mate_c[r], :, ck(k)], FR.at[s, :, ck(k)],
            f_s.at[k, r], f_r.at[k, r], mate_dev[r],
        )

    def h_copy(i, p=0):
        if i == 0:
            ref = HQ.at[s]
        else:
            ref = HQ.at[s if i == 1 else mate_s[1], pl.ds(p * 96, 96)]
        return Copy((h_copy, i, p), ref, ref, h_s.at[i, p], h_r.at[i, p], mate_dev[1 if i == 1 else 0])

    def w_copy(r):
        src = WB.at[:, cols(mate_s[r] * QW, QW)]
        return Copy((w_copy, r), src, WQ.at[x, zh, c], w_s.at[r], w_r.at[r], mate_dev[r])

    half = QW // 2
    pair = pl.ds(px * 2, 2)

    def ring_blk(i):
        return (zh + 3 + 2 * i) % 4

    def half_cols(i):
        return pl.ds(i * half, half)

    def wz_copy(p, i):
        ref = WQ.at[pair, zh, :, :, half_cols((i + p) % 2)]
        return Copy((wz_copy, p, i), ref, ref, wz_s.at[p, i], wz_r.at[p, i], ring_dev[i])

    def wf_copy(i):
        ref = WQ.at[pair, ring_blk(i), :, :, half_cols(i)]
        return Copy((wf_copy, i), ref, ref, wf_s.at[i], wf_r.at[i], ring_dev[i])

    def wx_copy(d):
        ref = WQ.at[pair, (zh + d) % 4]
        return Copy((wx_copy, d), ref, ref, wx_s.at[d], wx_r.at[d], xc_dev)

    def wp_copy(p, i):
        ref = WQ.at[pair, ring_blk(i), :, :, half_cols((i + p) % 2)]
        return Copy((wp_copy, p, i), ref, ref, wp_s.at[p, i], wp_r.at[p, i], xc_dev)

    NB = 4
    BW = 1024 // NB

    def slab_cols(u):
        n = (px * 2 if u < 2 else 2 - px * 2) + u % 2
        return cols(n * BW, BW)

    def g1_copy(i, u):
        sl = slab_cols(u)
        return Copy(
            (g1_copy, i, u), GS1.at[i, :, sl], GR1.at[i, :, sl], g1_s.at[i, u], g1_r.at[i, u], mate_dev[0]
        )

    def g2_copy(u):
        sl = slab_cols(u)
        return Copy((g2_copy, u), GX.at[:, sl], GR2.at[:, sl], g2_s.at[u], g2_r.at[u], mate_dev[1])

    def b_copy(i):
        return Copy((b_copy, i), RG.at[peer_ex[i]], BK.at[ex], b_s.at[i], b_r.at[i], peer_dev[i])

    def loads():
        return [
            pltpu.make_async_copy(g_ref.at[:, cols(s * QW, QW)], T.at[zl, s], l_s.at[0]),
            pltpu.make_async_copy(mas_hbm, MAS, l_s.at[1]),
            pltpu.make_async_copy(hid_hbm, HID, l_s.at[2]),
        ]

    barrier = pltpu.get_barrier_semaphore()
    everyone = mate_dev + [xc_dev] + peer_dev + zh_dev
    for to in everyone:
        pl.semaphore_signal(barrier, inc=1, device_id=to, device_id_type=MESH)
    for cp in loads():
        cp.start()

    sub = lax.broadcasted_iota(jnp.int32, (8, 128), 0).astype(F32)
    ids0, ids1 = ids_ref[0:1, :].astype(F32), ids_ref[1:2, :].astype(F32)
    prob = prob_ref[...].astype(F32)
    oh0 = (sub == ids0).astype(F32)
    oh1 = (sub == ids1).astype(F32)
    tri = (
        lax.broadcasted_iota(jnp.int32, (128, 128), 0) < lax.broadcasted_iota(jnp.int32, (128, 128), 1)
    ).astype(BF16)
    before = jnp.dot((oh0 + oh1).astype(BF16), tri, preferred_element_type=F32)
    t0 = ids0 * float(CAP) + jnp.sum(oh0 * before, axis=0, keepdims=True)
    t1 = ids1 * float(CAP) + jnp.sum(oh1 * before, axis=0, keepdims=True)
    mine = jnp.where(
        sub == 0.0, t0, jnp.where(sub == 1.0, t1, jnp.where(sub == 2.0, prob[0:1, :], prob[1:2, :]))
    )
    INF[zl, s] = mine
    INE[ex] = mine

    pl.semaphore_wait(barrier, len(everyone))

    def stage_info():
        for r in (1, 2, 0):
            info_mate(r).start()

    def stage_peer():
        for i in range(7):
            info_peer(i).start()

    def stage_w0():
        loads()[1].wait()
        WB[...] = MAS[...].astype(BF16)
        for r in (1, 2, 0):
            w_copy(r).start()
        WQ[x, zh, c] = WB[:, cols(s * QW, QW)]

    def stage_q(k):
        for r in (1, 2, 0):
            q_copy(k, r).start()

    def onehot(zz):
        rows = lax.broadcasted_iota(jnp.int32, (4 * CAP, 128), 0) + zl * (4 * CAP)
        rows = rows.astype(F32)
        for ss in range(4):
            inf = INF[zz, ss]
            hit = (rows == inf[0:1, :]) | (rows == inf[1:2, :])
            SO[zz, ss] = jnp.where(hit, 1.0, 0.0).astype(BF16)

    def stage_o0():
        for r in range(3):
            info_mate(r).wait_recv()
        info_z().start()
        onehot(zl)

    def stage_o1():
        info_z().wait_recv()
        onehot(1 - zl)

    def stage_h():
        for i in range(7):
            info_peer(i).wait_recv()
        loads()[2].wait()
        rows = (lax.broadcasted_iota(jnp.int32, (CAP, 128), 0) + ex * CAP).astype(F32)
        for j in range(8):
            inf = INE[j]
            w = jnp.where(rows == inf[0:1, :], inf[2:3, :], 0.0) + jnp.where(
                rows == inf[1:2, :], inf[3:4, :], 0.0
            )
            p = jnp.sum(w, axis=1, keepdims=True)
            PC[j * CAP:(j + 1) * CAP, :] = jnp.broadcast_to(p, (CAP, 128))
            HQ[s, j * CAP:(j + 1) * CAP, :] = (
                HID[j * CAP:(j + 1) * CAP, :].astype(F32) * p
            ).astype(BF16)
        h_copy(0).start()

    def stage_hp(p):
        h_copy(1, p).start()

    def stage_hf():
        for p in range(4):
            h_copy(1, p).wait_recv()
            h_copy(2, p).start()

    def stage_ht():
        h_copy(0).wait_recv()
        for p in range(4):
            h_copy(2, p).wait_recv()
        for ss in range(4):
            HT[:, ss * 384:(ss + 1) * 384] = HQ[ss].T

    def stage_b(k):
        for r in range(3):
            q_copy(k, r).wait_recv()
        if k == 0:
            loads()[0].wait()
        z_copy(k).start()

    def dispatch(k, o):
        zz = zl if o == 0 else 1 - zl
        for ss in range(4):
            out = jnp.dot(SO[zz, ss], T[zz, ss, :, ck(k)], preferred_element_type=F32).astype(BF16)
            for yy in range(4):
                SB[zz, yy, ss, :, ck(k)] = out[yy * CAP:(yy + 1) * CAP]
        for d in (2, 1, 3):
            y_copy(k, o, d).start()
        y_own(k, o).start()
        own.append((k, o))

    def stage_a(k):
        dispatch(k, 0)

    def stage_c(k):
        z_copy(k).wait_recv()
        dispatch(k, 1)

    def stage_d(k):
        for o in range(2):
            y_own(k, o).wait()
            own.remove((k, o))
            for d in (1, 2, 3):
                y_copy(k, o, d).wait_recv()
        rb = RB[:, :, :, :, ck(k)].reshape(4 * 384, WIDTHS[k])
        there = jnp.dot(HT[pl.ds((1 - px) * 512, 512), :], rb, preferred_element_type=F32)
        PX[:, ck(k)] = there.astype(BF16)
        x_copy(k).start()
        PO[:, ck(k)] = jnp.dot(HT[pl.ds(px * 512, 512), :], rb, preferred_element_type=F32)

    def stage_e(k):
        x_copy(k).wait_recv()
        tot = (PO[:, ck(k)] + XR[:, ck(k)].astype(F32)).astype(BF16).reshape(2, 4, 64, WIDTHS[k])
        for a in range(2):
            for b in range(4):
                ZS[b, a, :, ck(k)] = tot[a, b]
        if k in RING:
            for i in range(2):
                zr_copy(k, i).start()
            for i in range(2):
                zn_copy(k, i).start()
        else:
            for d in (2, 1, 3):
                zh_copy(k, d).start()

    def stage_e2(k):
        for i in range(2):
            zr_copy(k, i).wait_recv()
            blk = (zh + 1 + 2 * i) % 4
            tot = ZS[blk, i, :, ck(k)].astype(F32) + ZH[i, :, ck(k)].astype(F32)
            ZS[blk, i, :, ck(k)] = tot.astype(BF16)
            za_copy(k, i).start()

    def stage_f(k):
        if k in RING:
            for i in range(2):
                zn_copy(k, i).wait_recv()
                za_copy(k, i).wait_recv()
        else:
            for d in (1, 2, 3):
                zh_copy(k, d).wait_recv()
        tot = ZS[zh, :, :, ck(k)].astype(F32)
        for d in range(2 if k in RING else 3):
            tot = tot + ZR[d, :, :, ck(k)].astype(F32)
        FS[:, :, :, ck(k)] = tot.astype(BF16).reshape(2, 2, 32, WIDTHS[k])
        for r in (1, 2, 0):
            f_copy(k, r).start()
        FR[s, :, ck(k)] = FS[xl, c, :, ck(k)]

    def quad_weights():
        for r in range(3):
            if (w_copy, r) not in got:
                w_copy(r).wait_recv()

    def stage_w1():
        quad_weights()
        wx_copy(0).start()

    def stage_wa():
        quad_weights()
        for i in range(2):
            wz_copy(0, i).start()

    def stage_wb():
        for i in range(2):
            wz_copy(1, i).start()

    def stage_w2():
        for i in range(2):
            wz_copy(0, i).wait_recv()
            wf_copy(i).start()

    def stage_w2x():
        for i in range(2):
            wp_copy(0, i).start()

    def stage_w2y():
        for i in range(2):
            wz_copy(1, i).wait_recv()
            wp_copy(1, i).start()

    def stage_w3():
        for i in range(2):
            wf_copy(i).wait_recv()
        wx_copy(2).start()

    def stage_w4():
        for d in (0, 2):
            wx_copy(d).wait_recv()
        for p in range(2):
            for i in range(2):
                wp_copy(p, i).wait_recv()

    def stage_dr(k):
        for r in range(3):
            q_copy(k, r).wait_send()
        z_copy(k).wait_send()
        for o in range(2):
            for d in (1, 2, 3):
                y_copy(k, o, d).wait_send()

    def stage_ds(k):
        x_copy(k).wait_send()
        if k in RING:
            for i in range(2):
                zr_copy(k, i).wait_send()
                zn_copy(k, i).wait_send()
        else:
            for d in (1, 2, 3):
                zh_copy(k, d).wait_send()

    def stage_dw():
        info_z().wait_send()
        for r in range(3):
            info_mate(r).wait_send()
            w_copy(r).wait_send()
        h_copy(0).wait_send()
        for p in range(4):
            h_copy(1, p).wait_send()
            h_copy(2, p).wait_send()
        for i in range(7):
            info_peer(i).wait_send()
        for i in range(2):
            wz_copy(0, i).wait_send()
            wz_copy(1, i).wait_send()
            wf_copy(i).wait_send()

    nt = (((1,), (1,)), ((), ()))

    def gdot(row, n):
        wn = WQ[n].reshape(BW, QW)
        return lax.dot_general(RB[row].reshape(384, QW), wn, nt, preferred_element_type=F32)

    def blk(i):
        return [i * 2, i * 2 + 1], [(px * 2 if i == 0 else 2 - px * 2) + a for a in range(2)]

    def stage_g1(i):
        for u, n in zip(*blk(i)):
            sl = cols(n * BW, BW)
            GS1[0, :, sl] = gdot(mate_s[2], n).astype(BF16)
            g1_copy(0, u).start()
            GO1[:, sl] = gdot(mate_s[1], n)

    def stage_g2(i):
        for u, n in zip(*blk(i)):
            sl = cols(n * BW, BW)
            g1_copy(0, u).wait_recv()
            GX[:, sl] = (GO1[:, sl] + GR1[0, :, sl].astype(F32)).astype(BF16)
            g2_copy(u).start()

    def stage_g3():
        for i in range(2):
            for u, n in zip(*blk(i)):
                sl = cols(n * BW, BW)
                GS1[1, :, sl] = gdot(mate_s[0], n).astype(BF16)
                g1_copy(1, u).start()
                GO[:, sl] = gdot(s, n)

    def stage_gr():
        for n in range(NB):
            g1_copy(1, n).wait_recv()
        for n in range(NB):
            g2_copy(n).wait_recv()
        for j in range(8):
            sl = slice(j * CAP, (j + 1) * CAP)
            tot = GO[sl, :] + GR1[1, sl, :].astype(F32) + GR2[sl, :].astype(F32)
            rg = jnp.sum(HID[sl, :].astype(F32) * tot, axis=1, keepdims=True)
            RG[j] = jnp.broadcast_to(rg, (CAP, 128))
            gh_ref[sl, :] = (tot * PC[sl, 0:1]).astype(BF16)
        for i in range(7):
            b_copy(i).start()
        BK[ex] = RG[ex]

    def stage_gp():
        for i in range(7):
            b_copy(i).wait_recv()
        inf = INE[ex]
        acc0 = jnp.zeros((1, 128), F32)
        acc1 = jnp.zeros((1, 128), F32)
        base = lax.broadcasted_iota(jnp.int32, (CAP, 128), 0).astype(F32)
        for e in range(8):
            rows = base + float(e * CAP)
            acc0 += jnp.sum(jnp.where(rows == inf[0:1, :], BK[e], 0.0), axis=0, keepdims=True)
            acc1 += jnp.sum(jnp.where(rows == inf[1:2, :], BK[e], 0.0), axis=0, keepdims=True)
        gp_ref[0:1, :] = acc0
        gp_ref[1:2, :] = acc1

    def stage_end():
        for k in range(NC):
            for r in range(3):
                f_copy(k, r).wait_recv()
        for q in range(4):
            gr_ref[:, q * QW:(q + 1) * QW] = FR[q]

    fns = dict(
        info=stage_info, peer=stage_peer, w0=stage_w0, q=stage_q, o0=stage_o0, o1=stage_o1, h=stage_h, hp=stage_hp, hf=stage_hf, ht=stage_ht, a=stage_a, b=stage_b,
        c=stage_c, d=stage_d, e=stage_e, f=stage_f, w1=stage_w1, w2=stage_w2, w3=stage_w3, wa=stage_wa, wb=stage_wb, w2x=stage_w2x, w2y=stage_w2y,
        e2=stage_e2, dr=stage_dr, ds=stage_ds, dw=stage_dw,
        w4=stage_w4, g1=stage_g1, g2=stage_g2, g3=stage_g3, gr=stage_gr, gp=stage_gp, end=stage_end,
    )
    for name, *k in ORDER:
        fns[name](*k)

    for k in own:
        y_own(*k).wait()
    names = [item[0] for item in ORDER]
    for i, name in enumerate(("b", "w0", "h")):
        if name not in names:
            loads()[i].wait()
    for fn, *a in started:
        if (fn, *a) not in got:
            fn(*a).wait_recv()
        if (fn, *a) not in sent:
            fn(*a).wait_send()


ORDER = [
    ("q", 0), ("info",), ("q", 1), ("w0",), ("q", 2), ("q", 3), ("q", 4), ("q", 5), ("b", 0),
    ("peer",), ("q", 6), ("o0",), ("b", 1), ("a", 0), ("wa",), ("w1",), ("a", 1), ("o1",),
    ("wb",), ("h",), ("hp", 0), ("hp", 1), ("c", 0), ("b", 2), ("c", 1), ("b", 3), ("b", 4),
    ("a", 2), ("b", 5), ("a", 4), ("hp", 2), ("b", 6), ("hp", 3), ("w2",), ("w2x",), ("a", 3),
    ("w2y",), ("q", 7), ("c", 2), ("hf",), ("a", 6), ("ht",), ("d", 1), ("c", 3), ("d", 0),
    ("a", 5), ("b", 7), ("d", 2), ("c", 5), ("e", 1), ("d", 3), ("e", 0), ("c", 6), ("c", 4),
    ("e", 2), ("d", 5), ("a", 7), ("w3",), ("d", 6), ("c", 7), ("e2", 1), ("e", 3), ("d", 4),
    ("e", 5), ("d", 7), ("g1", 0), ("f", 1), ("e2", 0), ("e2", 2), ("g2", 0), ("e2", 3),
    ("w4",), ("g1", 1), ("e", 6), ("e2", 5), ("g2", 1), ("f", 0), ("f", 2), ("g3",), ("e", 4),
    ("f", 6), ("f", 3), ("f", 5), ("e", 7), ("e2", 4), ("gr",), ("f", 7), ("f", 4), ("gp",),
    ("end",),
]


def per_device(grad_output, hidden, probs, expert_ids, master, first_moment, second_moment):
    width = grad_output.shape[1]
    qw = width // 4
    nc = len(WIDTHS)
    slab = hidden.shape[4]
    rows = hidden.shape[2] * hidden.shape[3]
    vm = pl.BlockSpec(memory_space=pltpu.VMEM)
    hbm = pl.BlockSpec(memory_space=pl.ANY)
    dma = pltpu.SemaphoreType.DMA
    scratch = [
        pltpu.VMEM((2, 4, 8, 128), F32),
        pltpu.VMEM((8, 8, 128), F32),
        pltpu.VMEM((2, 4, 128, qw), BF16),
        pltpu.VMEM((2, 4, 4 * CAP, 128), BF16),
        pltpu.VMEM((2, 4, 4, CAP, qw), BF16),
        pltpu.VMEM((4, 2, 4, CAP, qw), BF16),
        pltpu.VMEM((rows, 128), F32),
        pltpu.VMEM((rows, slab), BF16),
        pltpu.VMEM((32, width), F32),
        pltpu.VMEM((4, rows, slab), BF16),
        pltpu.VMEM((slab, 4 * rows), BF16),
        pltpu.VMEM((32, width), BF16),
        pltpu.VMEM((4, 4, 2, 32, qw), BF16),
        pltpu.VMEM((512, qw), BF16),
        pltpu.VMEM((512, qw), F32),
        pltpu.VMEM((512, qw), BF16),
        pltpu.VMEM((4, 2, 64, qw), BF16),
        pltpu.VMEM((3, 2, 64, qw), BF16),
        pltpu.VMEM((2, 64, qw), BF16),
        pltpu.VMEM((2, 2, 32, qw), BF16),
        pltpu.VMEM((4, 32, qw), BF16),
        pltpu.VMEM((2, rows, slab), BF16),
        pltpu.VMEM((2, rows, slab), BF16),
        pltpu.VMEM((rows, slab), F32),
        pltpu.VMEM((rows, slab), BF16),
        pltpu.VMEM((rows, slab), BF16),
        pltpu.VMEM((rows, slab), F32),
        pltpu.VMEM((8, CAP, 128), F32),
        pltpu.VMEM((8, CAP, 128), F32),
        dma((3,)),
        dma((3,)), dma((3,)), dma((7,)), dma((7,)), dma, dma,
        dma((nc, 3)), dma((nc, 3)), dma((nc,)), dma((nc,)),
        dma((nc, 2, 3)), dma((nc, 2, 3)), dma((nc, 2)),
        dma((nc,)), dma((nc,)), dma((nc, 3)), dma((nc, 3)),
        dma((nc, 2)), dma((nc, 2)), dma((nc, 2)), dma((nc, 2)), dma((nc, 3)), dma((nc, 3)),
        dma((3, 4)), dma((3, 4)), dma((3,)), dma((3,)),
        dma((2, 2)), dma((2, 2)), dma((2,)), dma((2,)), dma((4,)), dma((4,)),
        dma((2, 2)), dma((2, 2)),
        dma((2, 4)), dma((2, 4)), dma((4,)), dma((4,)), dma((7,)), dma((7,)),
    ]
    gh, gp, gr = pl.pallas_call(
        kernel,
        out_shape=(
            jax.ShapeDtypeStruct((rows, slab), BF16),
            jax.ShapeDtypeStruct((2, 128), F32),
            jax.ShapeDtypeStruct((32, width), BF16),
        ),
        in_specs=[vm, vm, hbm, hbm, hbm],
        out_specs=(vm, vm, vm),
        scratch_shapes=scratch,
        compiler_params=pltpu.CompilerParams(
            collective_id=0, has_side_effects=True, vmem_limit_bytes=60 * 1024 * 1024
        ),
        cost_estimate=pl.CostEstimate(
            flops=10 * 10**9, bytes_accessed=8 * 10**6, transcendentals=0
        ),
    )(expert_ids.T, probs.T, grad_output, hidden.reshape(rows, slab), master.reshape(32, width))
    grad_hidden = gh.reshape(hidden.shape)
    grad_probs = gp.T
    grad = gr.astype(F32).reshape(master.shape)
    new_first = 0.9 * first_moment + 0.1 * grad
    new_second = 0.95 * second_moment + 0.05 * grad * grad
    first_hat = new_first / (1.0 - 0.9**50)
    second_hat = new_second / (1.0 - 0.95**50)
    new_master = master - 0.0003 * (first_hat / (jnp.sqrt(second_hat) + 1e-08) + 0.1 * master)
    return (grad_hidden, grad_probs, new_master, new_first, new_second)


def solution(mesh):
    in_specs = (
        P(("dp", "expert"), None),
        P("dp", "expert", None, None, None),
        P(("dp", "expert"), None),
        P(("dp", "expert"), None),
        P("expert", "dp", None),
        P("expert", "dp", None),
        P("expert", "dp", None),
    )
    out_specs = (
        P("dp", "expert", None, None, None),
        P(("dp", "expert"), None),
        P("expert", "dp", None),
        P("expert", "dp", None),
        P("expert", "dp", None),
    )
    return jax.shard_map(
        per_device, mesh=mesh, in_specs=in_specs, out_specs=out_specs, check_vma=False
    )
```
